256 devices in a mesh: seq: 8 (over x, core), ctx: 32 (over y, z).
Axes of the slice: x: 4, y: 4, z: 8, core: 2. Of those that a mesh axis runs over, the one named last changes fastest.
Arguments:
- queries: bfloat16 [65536, 2048], P(('seq', 'ctx')), parts along dimension 0, may hold values from -216 to 216
- keys: bfloat16 [65536, 512], P(('seq', 'ctx')), parts along dimension 0, may hold values from -6 to 6
- values: bfloat16 [65536, 512], P(('seq', 'ctx')), parts along dimension 0, may hold values from -6 to 6
- out_grad: bfloat16 [65536, 2048], P(('seq', 'ctx')), parts along dimension 0, may hold values from -6 to 6
- block_docs: int32 [512], P('seq'), parts along dimension 0, may hold values from 0 to 31, never falling along the last dimension, each value on 1 to 4 neighbouring positions
Outputs:
- attended: bfloat16 [65536, 2048], P(('seq', 'ctx')), parts along dimension 0
- query_grad: bfloat16 [65536, 2048], P(('seq', 'ctx')), parts along dimension 0
- key_grad: bfloat16 [65536, 512], P(('seq', 'ctx')), parts along dimension 0
- value_grad: bfloat16 [65536, 512], P(('seq', 'ctx')), parts along dimension 0
The draws below stay inside these ranges and needn't reach their ends.
There are 8 independent parts, one for each index of `seq`. The reference program is written for one: setup_inputs(seed, part) draws one part's arguments, and reference() takes and returns one part's arrays. A program takes and returns all parts, laid end to end along the dimension named above; each array names one. Nothing has to cross between parts.
Inputs may be any that keep to these rules, and one draw needn't show every extreme that they name: `block_docs`: documents are runs of 1 to 4 consecutive blocks, numbered from 0 and never falling; some document has exactly 4 blocks.
All inputs are finite; a program needn't handle non-finite values.
Results may differ from the reference program's by a relative error of at most 0.015.
Values may be sent and summed in bfloat16 or wider, within the bound.
A program may use at most 128 MiB of HBM per device.

```python
import math
import jax
import jax.numpy as jnp
import numpy as np
from jax import lax

HEAD_DIM = 128
HEADS = 16
KV_HEADS = 4
BLOCK = 128
MOST = 4
SEQ = 8192
BLOCKS = 64
DOCS = 32


def shared_base(key):
    base = jax.random.truncated_normal(key, -6.0, 6.0, (SEQ, KV_HEADS, HEAD_DIM), jnp.float32)
    return base


def draw_keys(key, part):
    base = shared_base(key)
    result = base
    return result.reshape(SEQ, KV_HEADS * HEAD_DIM).astype(jnp.bfloat16)


def draw_queries(key, part):
    key = jax.random.fold_in(key, 5)
    result = jax.random.truncated_normal(key, -6.0, 6.0, (SEQ, HEADS, HEAD_DIM), jnp.float32)
    return result.reshape(SEQ, HEADS * HEAD_DIM).astype(jnp.bfloat16)


def shard_levels(stream_key, shape, pieces, smallest, top_value):
    def one(dim, shards_of):
        heights = jax.random.uniform(jax.random.fold_in(jax.random.fold_in(stream_key, 6), dim), (shards_of,), jnp.float32, smallest / len(pieces), top_value / len(pieces))
        return jnp.repeat(jnp.exp(heights), shape[dim] // shards_of).reshape((-1,) + (1,) * (len(shape) - dim - 1))

    level = one(*pieces[0])
    for cut in pieces[1:]:
        level = level * one(*cut)
    return level


def length_profile(number_of, total, reach, skew):
    portions = [(1 << 20) // math.isqrt(grade ** skew) + 1 for grade in range(2, number_of + 1)]
    surplus, counts = total - reach - (number_of - 1), [1] * (number_of - 1)
    while surplus > 0:
        candidates = [i for i in range(number_of - 1) if counts[i] < reach]
        pool, budget = sum([portions[i] for i in candidates]), surplus
        for i in candidates:
            extra = min(reach - counts[i], max(1, budget * portions[i] // pool), surplus)
            counts[i] = counts[i] + extra
            surplus = surplus - extra
    return np.array([reach] + counts)


def ragged(key, amount, total, bound, skew):
    if amount == 2:
        one = jax.random.randint(key, (), max(1, total - bound), min(bound, total - 1) + 1)
        return jnp.stack([one, total - one])
    lengths = jnp.asarray(length_profile(amount, total, bound, skew), jnp.int32)
    couples = (amount - 1) // 2
    donor, taker = lengths[1:1 + 2 * couples:2], lengths[2:2 + 2 * couples:2]
    slack = jnp.minimum(donor - 1, bound - taker)
    moved = jax.random.randint(jax.random.fold_in(key, 1), (couples,), 0, 1 << 20) % (slack + 1)
    lengths = lengths.at[1:1 + 2 * couples:2].set(donor - moved).at[2:2 + 2 * couples:2].set(taker + moved)
    return lengths[jax.random.permutation(jax.random.fold_in(key, 2), amount)]


def gaussian(own_key, extent, scale, reach, split=(), held_as=jnp.bfloat16):
    values = scale * jax.random.normal(own_key, extent, jnp.float32)
    if split:
        values = values * shard_levels(own_key, extent, split, -0.22, 0.18)
    return jnp.clip(values, -reach, reach).astype(held_as)


def setup_inputs(seed: int = 0, part: int = 0) -> dict:
    key_list = jax.random.split(jax.random.key(seed), 6)
    part_splits = jax.random.split(jax.random.fold_in(key_list[5], part), 6)
    return {
        "queries": draw_queries(jax.random.fold_in(jax.random.fold_in(key_list[5], part), 71), part),
        "keys": draw_keys(jax.random.fold_in(jax.random.fold_in(key_list[5], part), 71), part),
        "values": gaussian(part_splits[2], (SEQ, KV_HEADS * HEAD_DIM), 1.0, 6.0, ((0, 32),)),
        "out_grad": gaussian(part_splits[3], (SEQ, HEADS * HEAD_DIM), 1.0, 6.0, ((0, 32),)),
        "block_docs": jnp.searchsorted(jnp.cumsum(ragged(part_splits[4], DOCS, BLOCKS, MOST, 2)), jnp.arange(BLOCKS), side="right").astype(jnp.int32),
    }


def rounded(array_in):
    return lax.optimization_barrier(array_in.astype(jnp.bfloat16)).astype(jnp.float32)

def reference(queries, keys, values, out_grad, block_docs):
    group_size = HEADS // KV_HEADS
    window_rows = MOST * BLOCK
    lead_rows = (MOST - 1) * BLOCK
    score_scale = 1.0 / math.sqrt(HEAD_DIM)
    blocks = SEQ // BLOCK
    kv_cols = KV_HEADS * HEAD_DIM
    key_pad = jnp.concatenate([jnp.zeros((lead_rows, kv_cols), keys.dtype), keys], 0)
    value_pad = jnp.concatenate([jnp.zeros((lead_rows, kv_cols), values.dtype), values], 0)
    doc_pad = jnp.concatenate([jnp.full((MOST - 1,), -1, jnp.int32), block_docs.astype(jnp.int32)])
    query_blocks = queries.reshape(blocks, BLOCK, KV_HEADS, group_size, HEAD_DIM)
    grad_blocks = out_grad.reshape(blocks, BLOCK, KV_HEADS, group_size, HEAD_DIM)
    row_ids = jnp.arange(BLOCK, dtype=jnp.int32)
    tile_of_key = jnp.arange(window_rows, dtype=jnp.int32) // BLOCK
    col_in_tile = jnp.arange(window_rows, dtype=jnp.int32) % BLOCK

    def one_block(sums_carry, block_index):
        key_acc, value_acc = sums_carry
        query_four = query_blocks[block_index].astype(jnp.float32)
        grad_four = grad_blocks[block_index].astype(jnp.float32)
        row_start = (block_index * BLOCK).astype(jnp.int32)
        key_window = lax.dynamic_slice_in_dim(key_pad, row_start, window_rows, 0)
        value_window = lax.dynamic_slice_in_dim(value_pad, row_start, window_rows, 0)
        tile_docs = lax.dynamic_slice_in_dim(doc_pad, block_index.astype(jnp.int32), MOST, 0)
        tile_live = tile_docs == block_docs[block_index]
        last_tile = tile_of_key == MOST - 1
        allowed = tile_live[tile_of_key][None, :] & (jnp.logical_not(last_tile)[None, :] | (col_in_tile[None, :] <= row_ids[:, None]))
        key_three = key_window.reshape(window_rows, KV_HEADS, HEAD_DIM).astype(jnp.float32)
        value_three = value_window.reshape(window_rows, KV_HEADS, HEAD_DIM).astype(jnp.float32)
        scores = jnp.einsum('qkgd,skd->kgqs', query_four, key_three) * score_scale
        scores = jnp.where(allowed, scores, -jnp.inf)
        row_top = lax.optimization_barrier(jnp.max(scores, axis=-1, keepdims=True))
        exponent = jnp.exp(scores - row_top)
        weights = exponent / lax.optimization_barrier(jnp.sum(exponent, axis=-1, keepdims=True))
        weights_b = rounded(weights)
        output = jnp.einsum('kgqs,skd->qkgd', weights_b, value_three).astype(jnp.bfloat16)
        row_dot = jnp.einsum('qkgd,qkgd->kgq', grad_four, output.astype(jnp.float32))
        weight_grad = jnp.einsum('qkgd,skd->kgqs', grad_four, value_three)
        score_grad = rounded(weights * (weight_grad - row_dot[..., None]))
        query_part = (jnp.einsum('kgqs,skd->qkgd', score_grad, key_three) * score_scale).astype(jnp.bfloat16)
        key_part = jnp.einsum('kgqs,qkgd->skd', score_grad, query_four) * score_scale
        value_part = jnp.einsum('kgqs,qkgd->skd', weights_b, grad_four)
        key_old = lax.dynamic_slice_in_dim(key_acc, row_start, window_rows, 0)
        key_acc = lax.dynamic_update_slice_in_dim(key_acc, key_old + key_part.reshape(window_rows, kv_cols), row_start, 0)
        value_old = lax.dynamic_slice_in_dim(value_acc, row_start, window_rows, 0)
        value_acc = lax.dynamic_update_slice_in_dim(value_acc, value_old + value_part.reshape(window_rows, kv_cols), row_start, 0)
        return ((key_acc, value_acc), (output.reshape(BLOCK, HEADS * HEAD_DIM), query_part.reshape(BLOCK, HEADS * HEAD_DIM)))
    start_sums = (jnp.zeros((lead_rows + SEQ, kv_cols), jnp.float32), jnp.zeros((lead_rows + SEQ, kv_cols), jnp.float32))
    (key_acc, value_acc), (outputs, query_parts) = lax.scan(one_block, start_sums, jnp.arange(blocks, dtype=jnp.int32))
    attended = outputs.reshape(SEQ, HEADS * HEAD_DIM)
    query_grad = query_parts.reshape(SEQ, HEADS * HEAD_DIM)
    return (attended, query_grad, key_acc[lead_rows:].astype(jnp.bfloat16), value_acc[lead_rows:].astype(jnp.bfloat16))
```

```python
import math

import jax
import jax.numpy as jnp
from jax import lax
from jax.experimental import pallas as pl
from jax.experimental.pallas import tpu as pltpu
from jax.sharding import PartitionSpec as P

HEAD_DIM = 128
HEADS = 16
KV_HEADS = 4
GROUP = HEADS // KV_HEADS
BLOCK = 128
MOST = 4
ROWS = 256
LEAD = (MOST - 1) * BLOCK
WINDOW = MOST * BLOCK
SCALE = 1.0 / math.sqrt(HEAD_DIM)
SCALE_LOG2 = math.log2(math.e) / math.sqrt(HEAD_DIM)
FAR = 1e30
MESH = pl.DeviceIdType.MESH

NT = (((1,), (1,)), ((), ()))
TN = (((0,), (0,)), ((), ()))
NN = (((1,), (0,)), ((), ()))


def dot(lhs, rhs, dims):
    return lax.dot_general(lhs, rhs, dims, preferred_element_type=jnp.float32)


def block_rows(value, index):
    return value[index * BLOCK : (index + 1) * BLOCK]


def attend(keys, values, queries, grads, live):
    scores = dot(keys, queries, NT)
    weight_grad = dot(values, grads, NT)
    width = queries.shape[0]
    key_ids = lax.broadcasted_iota(jnp.int32, (BLOCK, width), 0)
    query_ids = lax.broadcasted_iota(jnp.int32, (BLOCK, width), 1) % BLOCK
    tiles = [block_rows(scores, t) for t in range(MOST)]
    tiles[-1] = jnp.where(key_ids <= query_ids, tiles[-1], -FAR)
    top = jnp.max(tiles[-1], axis=0, keepdims=True)
    for t in range(MOST - 1):
        top = jnp.maximum(top, jnp.where(live[t], jnp.max(tiles[t], axis=0, keepdims=True), -FAR))
    top = top * SCALE_LOG2
    shifts = [jnp.where(live[t], top, FAR) for t in range(MOST - 1)] + [top]
    exps = [jnp.exp2(tiles[t] * SCALE_LOG2 - shifts[t]) for t in range(MOST)]
    total = sum(jnp.sum(part, axis=0, keepdims=True) for part in exps)
    weights = jnp.concatenate(exps, 0) * (1.0 / total)
    weights_b = weights.astype(jnp.bfloat16)
    row_dot = jnp.sum(weights * weight_grad, axis=0, keepdims=True)
    score_grad = (weights * (weight_grad - row_dot)).astype(jnp.bfloat16)
    attended = jnp.transpose(dot(values, weights_b, TN).astype(jnp.bfloat16))
    query_grad = jnp.transpose((dot(keys, score_grad, TN) * SCALE).astype(jnp.bfloat16))
    key_part = dot(score_grad, queries, NN) * SCALE
    value_part = dot(weights_b, grads, NN)
    return attended, query_grad, key_part, value_part


def kernel(
    docs, q_hbm, k_hbm, v_hbm, g_hbm, att_hbm, dq_hbm, dk_hbm, dv_hbm,
    q_buf, g_buf, kv_buf, att_buf, dq_buf, out_buf, part, own_part, send_buf, got_buf,
    load_sem, kv_sem, store_sem, out_sem,
    own_send, own_recv, fwd_send, fwd_recv, ret_send, ret_recv,
):
    seq = lax.axis_index("seq")
    me = lax.axis_index("ctx")
    last = lax.axis_size("ctx") - 1
    has_prev, has_next = me > 0, me < last
    prev, following = jnp.maximum(me - 1, 0), jnp.minimum(me + 1, last)

    barrier = pltpu.get_barrier_semaphore()

    @pl.when(has_prev)
    def _():
        pl.semaphore_signal(barrier, inc=1, device_id=(seq, prev), device_id_type=MESH)

    kv_loads = []
    for h in range(KV_HEADS):
        for n, ref in enumerate((k_hbm, v_hbm)):
            copy = pltpu.make_async_copy(
                ref.at[:, pl.ds(h * HEAD_DIM, HEAD_DIM)],
                kv_buf.at[h, n, pl.ds(LEAD, ROWS)],
                kv_sem.at[h, n],
            )
            copy.start()
            kv_loads.append(copy)
    loads = [
        pltpu.make_async_copy(q_hbm, q_buf, load_sem.at[0]),
        pltpu.make_async_copy(g_hbm, g_buf, load_sem.at[1]),
    ]
    for copy in loads:
        copy.start()

    def own(h, b):
        return pltpu.make_async_remote_copy(
            kv_buf.at[h, :, pl.ds(LEAD + b * BLOCK, BLOCK)],
            kv_buf.at[h, :, pl.ds((1 + b) * BLOCK, BLOCK)],
            own_send.at[h, b], own_recv.at[h, b],
            device_id=(seq, following), device_id_type=MESH,
        )

    def forward(h):
        return pltpu.make_async_remote_copy(
            kv_buf.at[h, :, pl.ds(2 * BLOCK, BLOCK)],
            kv_buf.at[h, :, pl.ds(0, BLOCK)],
            fwd_send.at[h], fwd_recv.at[h],
            device_id=(seq, following), device_id_type=MESH,
        )

    def give_back(h, b):
        return pltpu.make_async_remote_copy(
            send_buf.at[h, b], got_buf.at[h, b],
            ret_send.at[h, b], ret_recv.at[h, b],
            device_id=(seq, prev), device_id_type=MESH,
        )

    @pl.when(has_next)
    def _():
        pl.semaphore_wait(barrier, 1)

    for copy in kv_loads:
        copy.wait()

    @pl.when(has_next)
    def _():
        for h in range(2):
            own(h, 1).start()
            own(h, 0).start()

    @pl.when(jnp.logical_not(has_prev))
    def _():
        kv_buf[:, :, :LEAD] = jnp.zeros((KV_HEADS, 2, LEAD, HEAD_DIM), jnp.bfloat16)

    for copy in loads:
        copy.wait()

    def live(slot):
        own_doc = docs[2 * me + slot]
        result = []
        for t in range(MOST - 1):
            place = 2 * me + slot + t - (MOST - 1)
            result.append((place >= 0) & (docs[jnp.maximum(place, 0)] == own_doc))
        return result

    lives = [live(0), live(1)]

    def compute(h, slot):
        rows = slice(slot * BLOCK, (slot + 1) * BLOCK)
        lanes = [slice((h * GROUP + j) * HEAD_DIM, (h * GROUP + j + 1) * HEAD_DIM) for j in range(GROUP)]
        queries = jnp.concatenate([q_buf[rows, lane] for lane in lanes], 0)
        grads = jnp.concatenate([g_buf[rows, lane] for lane in lanes], 0)
        keys = kv_buf[h, 0, slot * BLOCK : slot * BLOCK + WINDOW]
        values = kv_buf[h, 1, slot * BLOCK : slot * BLOCK + WINDOW]
        attended, query_grad, key_part, value_part = attend(keys, values, queries, grads, lives[slot])
        for j, lane in enumerate(lanes):
            att_buf[rows, lane] = block_rows(attended, j)
            dq_buf[rows, lane] = block_rows(query_grad, j)
        return key_part, value_part

    def relay(h):
        @pl.when(has_next)
        def _():
            give_back(h, 0).wait_recv()
            part[h % 2] += got_buf[h, 0].astype(jnp.float32)

        @pl.when(has_prev)
        def _():
            send_buf[h, 2] = part[h % 2].astype(jnp.bfloat16)
            give_back(h, 2).start()

    def stores(h):
        lanes = pl.ds(h * HEAD_DIM, HEAD_DIM)
        return [
            pltpu.make_async_copy(out_buf.at[h, n], ref.at[:, lanes], out_sem.at[h, n])
            for n, ref in enumerate((dk_hbm, dv_hbm))
        ]

    def finish(h):
        @pl.when(has_next)
        def _():
            for b in range(2):
                give_back(h, 1 + b).wait_recv()
                own_part[h % 2, b] += got_buf[h, 1 + b].astype(jnp.float32)

        for n in range(2):
            for b in range(2):
                out_buf[h, n, b * BLOCK : (b + 1) * BLOCK] = own_part[h % 2, b, n].astype(jnp.bfloat16)
        for copy in stores(h):
            copy.start()

    wide = GROUP * HEAD_DIM

    def wide_stores(h):
        lanes = pl.ds(h * wide, wide)
        return [
            pltpu.make_async_copy(att_buf.at[:, lanes], att_hbm.at[:, lanes], store_sem.at[h, 0]),
            pltpu.make_async_copy(dq_buf.at[:, lanes], dq_hbm.at[:, lanes], store_sem.at[h, 1]),
        ]

    for h in range(KV_HEADS):

        @pl.when(has_prev)
        def _(h=h):
            own(h, 1).wait_recv()

        @pl.when(has_next)
        def _(h=h):
            forward(h).start()
            if h + 2 < KV_HEADS:
                own(h + 2, 1).start()
                own(h + 2, 0).start()

        @pl.when(has_prev)
        def _(h=h):
            own(h, 0).wait_recv()

        later = compute(h, 1)
        for n in range(2):
            part[h % 2, n] = block_rows(later[n], 1)
            own_part[h % 2, 0, n] = block_rows(later[n], 2)
            own_part[h % 2, 1, n] = block_rows(later[n], 3)
            send_f32 = block_rows(later[n], 0)
            own_part[h % 2, 2, n] = send_f32

        if h > 0:
            relay(h - 1)

        @pl.when(has_prev)
        def _(h=h):
            forward(h).wait_recv()

        earlier = compute(h, 0)
        for n in range(2):
            part[h % 2, n] += block_rows(earlier[n], 2)
            own_part[h % 2, 0, n] += block_rows(earlier[n], 3)
            send_buf[h, 0, n] = block_rows(earlier[n], 0).astype(jnp.bfloat16)
            send_buf[h, 1, n] = (block_rows(earlier[n], 1) + own_part[h % 2, 2, n]).astype(jnp.bfloat16)

        @pl.when(has_prev)
        def _(h=h):
            give_back(h, 0).start()
            give_back(h, 1).start()

        for copy in wide_stores(h):
            copy.start()
        if h > 0:
            finish(h - 1)

    relay(KV_HEADS - 1)
    finish(KV_HEADS - 1)

    @pl.when(has_next)
    def _():
        for h in range(KV_HEADS):
            own(h, 1).wait_send()
            own(h, 0).wait_send()
            forward(h).wait_send()

    @pl.when(has_prev)
    def _():
        for h in range(KV_HEADS):
            for b in range(3):
                give_back(h, b).wait_send()

    for h in range(KV_HEADS):
        for copy in wide_stores(h) + stores(h):
            copy.wait()


def on_device(queries, keys, values, out_grad, block_docs):
    hbm = pl.BlockSpec(memory_space=pl.ANY)
    dma = pltpu.SemaphoreType.DMA
    bf16, f32 = jnp.bfloat16, jnp.float32
    return pl.pallas_call(
        kernel,
        out_shape=[
            jax.ShapeDtypeStruct(queries.shape, bf16),
            jax.ShapeDtypeStruct(queries.shape, bf16),
            jax.ShapeDtypeStruct(keys.shape, bf16),
            jax.ShapeDtypeStruct(keys.shape, bf16),
        ],
        in_specs=[pl.BlockSpec(memory_space=pltpu.SMEM)] + [hbm] * 4,
        out_specs=[hbm] * 4,
        scratch_shapes=[
            pltpu.VMEM((ROWS, HEADS * HEAD_DIM), bf16),
            pltpu.VMEM((ROWS, HEADS * HEAD_DIM), bf16),
            pltpu.VMEM((KV_HEADS, 2, LEAD + ROWS, HEAD_DIM), bf16),
            pltpu.VMEM((ROWS, HEADS * HEAD_DIM), bf16),
            pltpu.VMEM((ROWS, HEADS * HEAD_DIM), bf16),
            pltpu.VMEM((KV_HEADS, 2, ROWS, HEAD_DIM), bf16),
            pltpu.VMEM((2, 2, BLOCK, HEAD_DIM), f32),
            pltpu.VMEM((2, 3, 2, BLOCK, HEAD_DIM), f32),
            pltpu.VMEM((KV_HEADS, 3, 2, BLOCK, HEAD_DIM), bf16),
            pltpu.VMEM((KV_HEADS, 3, 2, BLOCK, HEAD_DIM), bf16),
            dma((2,)),
            dma((KV_HEADS, 2)),
            dma((KV_HEADS, 2)),
            dma((KV_HEADS, 2)),
            dma((KV_HEADS, 2)),
            dma((KV_HEADS, 2)),
            dma((KV_HEADS,)),
            dma((KV_HEADS,)),
            dma((KV_HEADS, 3)),
            dma((KV_HEADS, 3)),
        ],
        compiler_params=pltpu.CompilerParams(
            collective_id=0, has_side_effects=True, vmem_limit_bytes=62 * 1024 * 1024
        ),
        cost_estimate=pl.CostEstimate(
            flops=3_300_000_000, bytes_accessed=5_500_000, transcendentals=2_100_000
        ),
    )(block_docs, queries, keys, values, out_grad)


def solution(mesh):
    tokens = P(("seq", "ctx"), None)
    return jax.shard_map(
        on_device,
        mesh=mesh,
        in_specs=(tokens, tokens, tokens, tokens, P("seq")),
        out_specs=(tokens, tokens, tokens, tokens),
        check_vma=False,
    )
```

```python
import math

import jax
import jax.numpy as jnp
from jax import lax
from jax.experimental import pallas as pl
from jax.experimental.pallas import tpu as pltpu
from jax.sharding import PartitionSpec as P

HEAD_DIM = 128
HEADS = 16
KV_HEADS = 4
GROUP = HEADS // KV_HEADS
BLOCK = 128
MOST = 4
PIECES = 4
PIECE = 64
ROWS = 256
LEAD = (MOST - 1) * BLOCK
WINDOW = MOST * BLOCK
SCALE = 1.0 / math.sqrt(HEAD_DIM)
SCALE_LOG2 = math.log2(math.e) / math.sqrt(HEAD_DIM)
FAR = 1e30
MESH = pl.DeviceIdType.MESH

NT = (((1,), (1,)), ((), ()))
TN = (((0,), (0,)), ((), ()))
NN = (((1,), (0,)), ((), ()))


def dot(lhs, rhs, dims):
    return lax.dot_general(lhs, rhs, dims, preferred_element_type=jnp.float32)


def block_rows(value, index):
    return value[index * BLOCK : (index + 1) * BLOCK]


def attend(keys, values, queries, grads, live):
    width = queries.shape[0]
    scores = dot(keys, queries, NT)
    weight_grad = dot(values, grads, NT)
    causal = lax.broadcasted_iota(jnp.int32, (BLOCK, BLOCK), 0) <= lax.broadcasted_iota(
        jnp.int32, (BLOCK, BLOCK), 1
    )
    exps, inverses = [], []
    for lane in range(0, width, BLOCK):
        tiles = [block_rows(scores, t)[:, lane : lane + BLOCK] for t in range(MOST)]
        tiles[-1] = jnp.where(causal, tiles[-1], -FAR)
        top = jnp.max(tiles[-1], axis=0, keepdims=True)
        for t in range(MOST - 1):
            top = jnp.maximum(top, jnp.where(live[t], jnp.max(tiles[t], axis=0, keepdims=True), -FAR))
        top = top * SCALE_LOG2
        shifts = [jnp.where(live[t], top, FAR) for t in range(MOST - 1)] + [top]
        parts = [jnp.exp2(tiles[t] * SCALE_LOG2 - shifts[t]) for t in range(MOST)]
        inverses.append(1.0 / jnp.sum(sum(parts), axis=0, keepdims=True))
        exps.append(jnp.concatenate([p.astype(jnp.bfloat16) for p in parts], 0))
    exps = jnp.concatenate(exps, 1)
    inverse = jnp.concatenate(inverses, 1)
    attended = dot(values, exps, TN) * inverse
    row_dot = jnp.sum(attended * jnp.transpose(grads).astype(jnp.float32), axis=0, keepdims=True)
    score_grad = []
    for lane in range(0, width, BLOCK):
        lanes = slice(lane, lane + BLOCK)
        score_grad.append(
            jnp.concatenate(
                [
                    block_rows(exps, t)[:, lanes]
                    * (block_rows(weight_grad, t)[:, lanes] - row_dot[:, lanes]).astype(jnp.bfloat16)
                    for t in range(MOST)
                ],
                0,
            )
        )
    score_grad = jnp.concatenate(score_grad, 1)
    column = jnp.transpose(jnp.broadcast_to(inverse, (BLOCK, width)))
    value_part = dot(exps, (grads.astype(jnp.float32) * column).astype(jnp.bfloat16), NN)
    key_part = dot(score_grad, (queries.astype(jnp.float32) * column).astype(jnp.bfloat16), NN)

    def outputs():
        query_grad = dot(keys, score_grad, TN) * (inverse * SCALE)
        return (
            jnp.transpose(attended.astype(jnp.bfloat16)),
            jnp.transpose(query_grad.astype(jnp.bfloat16)),
        )

    return key_part * SCALE, value_part, outputs


def kernel(
    docs_hbm, q_hbm, k_hbm, v_hbm, g_hbm, att_buf, dq_buf, dk_buf, dv_buf,
    docs, q_buf, g_buf, kv_buf, part, own_part, send_buf, got_buf,
    load_sem, kv_sem,
    first_send, first_recv, own_send, own_recv, fwd_send, fwd_recv, ret_send, ret_recv,
):
    seq = lax.axis_index("seq")
    me = lax.axis_index("ctx")
    last = lax.axis_size("ctx") - 1
    has_prev, has_next = me > 0, me < last
    prev, following = jnp.maximum(me - 1, 0), jnp.minimum(me + 1, last)

    barrier = pltpu.get_barrier_semaphore()

    @pl.when(has_prev)
    def _():
        pl.semaphore_signal(barrier, inc=1, device_id=(seq, prev), device_id_type=MESH)

    kv_loads = []
    for h in range(KV_HEADS):
        for n, ref in enumerate((k_hbm, v_hbm)):
            copy = pltpu.make_async_copy(
                ref.at[:, pl.ds(h * HEAD_DIM, HEAD_DIM)],
                kv_buf.at[h, n, pl.ds(LEAD, ROWS)],
                kv_sem.at[h, n],
            )
            copy.start()
            kv_loads.append(copy)
    loads = [
        pltpu.make_async_copy(q_hbm, q_buf, load_sem.at[0]),
        pltpu.make_async_copy(g_hbm, g_buf, load_sem.at[1]),
        pltpu.make_async_copy(docs_hbm, docs, load_sem.at[2]),
    ]
    for copy in loads:
        copy.start()

    def own(h, b):
        return pltpu.make_async_remote_copy(
            kv_buf.at[h, :, pl.ds(LEAD + b * BLOCK, BLOCK)],
            kv_buf.at[h, :, pl.ds((1 + b) * BLOCK, BLOCK)],
            own_send.at[h, b], own_recv.at[h, b],
            device_id=(seq, following), device_id_type=MESH,
        )

    def first(p):
        n, rows = p // 2, p % 2 * PIECE
        return pltpu.make_async_remote_copy(
            (k_hbm, v_hbm)[n].at[pl.ds(BLOCK + rows, PIECE), pl.ds(0, HEAD_DIM)],
            kv_buf.at[0, n, pl.ds(2 * BLOCK + rows, PIECE)],
            first_send.at[p], first_recv.at[p],
            device_id=(seq, following), device_id_type=MESH,
        )

    def forward(h):
        return pltpu.make_async_remote_copy(
            kv_buf.at[h, :, pl.ds(2 * BLOCK, BLOCK)],
            kv_buf.at[h, :, pl.ds(0, BLOCK)],
            fwd_send.at[h], fwd_recv.at[h],
            device_id=(seq, following), device_id_type=MESH,
        )

    def forward_first(p):
        n, rows = p // 2, p % 2 * PIECE
        return pltpu.make_async_remote_copy(
            kv_buf.at[0, n, pl.ds(2 * BLOCK + rows, PIECE)],
            kv_buf.at[0, n, pl.ds(rows, PIECE)],
            first_send.at[PIECES + p], first_recv.at[PIECES + p],
            device_id=(seq, following), device_id_type=MESH,
        )

    def give_back(h, b, n):
        return pltpu.make_async_remote_copy(
            send_buf.at[h, b, n], got_buf.at[h, b, n],
            ret_send.at[h, b, n], ret_recv.at[h, b, n],
            device_id=(seq, prev), device_id_type=MESH,
        )

    def next_first(h):
        @pl.when(has_next)
        def _():
            own(h, 1).start()

    def next_second(h):
        @pl.when(has_next)
        def _():
            own(h, 0).start()

    @pl.when(has_next)
    def _():
        pl.semaphore_wait(barrier, 1)
        for p in range(PIECES):
            first(p).start()

    for copy in kv_loads:
        copy.wait()

    next_second(0)

    @pl.when(jnp.logical_not(has_prev))
    def _():
        kv_buf[:, :, :LEAD] = jnp.zeros((KV_HEADS, 2, LEAD, HEAD_DIM), jnp.bfloat16)

    for copy in loads:
        copy.wait()

    def live(slot):
        own_doc = docs[2 * me + slot]
        result = []
        for t in range(MOST - 1):
            place = 2 * me + slot + t - (MOST - 1)
            result.append((place >= 0) & (docs[jnp.maximum(place, 0)] == own_doc))
        return result

    lives = [live(0), live(1)]

    def compute(h, slot):
        rows = slice(slot * BLOCK, (slot + 1) * BLOCK)
        lanes = [slice((h * GROUP + j) * HEAD_DIM, (h * GROUP + j + 1) * HEAD_DIM) for j in range(GROUP)]
        queries = jnp.concatenate([q_buf[rows, lane] for lane in lanes], 0)
        grads = jnp.concatenate([g_buf[rows, lane] for lane in lanes], 0)
        keys = kv_buf[h, 0, slot * BLOCK : slot * BLOCK + WINDOW]
        values = kv_buf[h, 1, slot * BLOCK : slot * BLOCK + WINDOW]
        key_part, value_part, outputs = attend(keys, values, queries, grads, lives[slot])

        def write():
            attended, query_grad = outputs()
            for j, lane in enumerate(lanes):
                att_buf[rows, lane] = block_rows(attended, j)
                dq_buf[rows, lane] = block_rows(query_grad, j)

        return (key_part, value_part), write

    def relay(h):
        @pl.when(has_next)
        def _():
            for n in (1, 0):
                give_back(h, 0, n).wait_recv()
                send_buf[h, 2, n] = (part[h, n] + got_buf[h, 0, n].astype(jnp.float32)).astype(jnp.bfloat16)

                @pl.when(has_prev)
                def _(n=n):
                    give_back(h, 2, n).start()

        @pl.when(jnp.logical_not(has_next))
        def _():
            send_buf[h, 2] = part[h].astype(jnp.bfloat16)
            for n in (1, 0):
                give_back(h, 2, n).start()

    def finish(h):
        @pl.when(has_next)
        def _():
            for b in range(2):
                for n in range(2):
                    give_back(h, 1 + b, n).wait_recv()
                own_part[h, b] += got_buf[h, 1 + b].astype(jnp.float32)

        for n, ref in enumerate((dk_buf, dv_buf)):
            for b in range(2):
                ref[b * BLOCK : (b + 1) * BLOCK, h * HEAD_DIM : (h + 1) * HEAD_DIM] = own_part[
                    h, b, n
                ].astype(jnp.bfloat16)

    def pass_on(h):
        if h == 0:
            for p in range(PIECES):

                @pl.when(has_prev)
                def _(p=p):
                    first(p).wait_recv()

                @pl.when(has_next)
                def _(p=p):
                    forward_first(p).start()
        else:

            @pl.when(has_prev)
            def _():
                own(h, 1).wait_recv()

            @pl.when(has_next)
            def _():
                forward(h).start()

    def slot_one(h):
        @pl.when(has_prev)
        def _():
            own(h, 0).wait_recv()

        sums, write = compute(h, 1)
        for n in range(2):
            part[h, n] = block_rows(sums[n], 1)
            own_part[h, 0, n] = block_rows(sums[n], 2)
            own_part[h, 1, n] = block_rows(sums[n], 3)
            own_part[h, 2, n] = block_rows(sums[n], 0)
        write()

    def slot_zero(h):
        @pl.when(has_prev)
        def _():
            if h == 0:
                for p in range(PIECES):
                    forward_first(p).wait_recv()
            else:
                forward(h).wait_recv()

        sums, write = compute(h, 0)
        for n in range(2):
            send_buf[h, 0, n] = block_rows(sums[n], 0).astype(jnp.bfloat16)
            send_buf[h, 1, n] = (block_rows(sums[n], 1) + own_part[h, 2, n]).astype(jnp.bfloat16)

        @pl.when(has_prev)
        def _():
            for b in range(2):
                for n in (1, 0):
                    give_back(h, b, n).start()

        for n in range(2):
            part[h, n] += block_rows(sums[n], 2)
            own_part[h, 0, n] += block_rows(sums[n], 3)
        write()

    order = (
        (next_first, 1),
        (pass_on, 0),
        (next_first, 2),
        (next_second, 1),
        (pass_on, 1),
        (next_second, 2),
        (next_first, 3),
        (slot_one, 0),
        (slot_zero, 0),
        (pass_on, 2),
        (slot_one, 1),
        (slot_zero, 1),
        (next_second, 3),
        (slot_one, 2),
        (pass_on, 3),
        (relay, 0),
        (slot_zero, 2),
        (slot_one, 3),
        (slot_zero, 3),
        (relay, 1),
        (relay, 2),
        (relay, 3),
        (finish, 2),
        (finish, 1),
        (finish, 0),
        (finish, 3),
    )
    for step, h in order:
        step(h)

    @pl.when(has_next)
    def _():
        for p in range(PIECES):
            first(p).wait_send()
            forward_first(p).wait_send()
        for h in range(KV_HEADS):
            own(h, 0).wait_send()
            if h > 0:
                own(h, 1).wait_send()
                forward(h).wait_send()

    @pl.when(has_prev)
    def _():
        for h in range(KV_HEADS):
            for b in range(3):
                for n in range(2):
                    give_back(h, b, n).wait_send()

def write_out(*refs):
    count = len(refs) // 2
    sem = refs[-1]
    copies = [pltpu.make_async_copy(refs[n], refs[count + n], sem.at[n]) for n in range(count)]
    for copy in copies:
        copy.start()
    for copy in copies:
        copy.wait()


def on_device(queries, keys, values, out_grad, block_docs):
    hbm = pl.BlockSpec(memory_space=pl.ANY)
    dma = pltpu.SemaphoreType.DMA
    bf16, f32 = jnp.bfloat16, jnp.float32
    vmem = pl.BlockSpec(memory_space=pltpu.VMEM)
    results = pl.pallas_call(
        kernel,
        out_shape=[
            pltpu.VMEM(queries.shape, bf16),
            pltpu.VMEM(queries.shape, bf16),
            pltpu.VMEM(keys.shape, bf16),
            pltpu.VMEM(keys.shape, bf16),
        ],
        in_specs=[hbm] * 5,
        out_specs=[vmem] * 4,
        scratch_shapes=[
            pltpu.SMEM(block_docs.shape, jnp.int32),
            pltpu.VMEM((ROWS, HEADS * HEAD_DIM), bf16),
            pltpu.VMEM((ROWS, HEADS * HEAD_DIM), bf16),
            pltpu.VMEM((KV_HEADS, 2, LEAD + ROWS, HEAD_DIM), bf16),
            pltpu.VMEM((KV_HEADS, 2, BLOCK, HEAD_DIM), f32),
            pltpu.VMEM((KV_HEADS, 3, 2, BLOCK, HEAD_DIM), f32),
            pltpu.VMEM((KV_HEADS, 3, 2, BLOCK, HEAD_DIM), bf16),
            pltpu.VMEM((KV_HEADS, 3, 2, BLOCK, HEAD_DIM), bf16),
            dma((3,)),
            dma((KV_HEADS, 2)),
            dma((2 * PIECES,)),
            dma((2 * PIECES,)),
            dma((KV_HEADS, 2)),
            dma((KV_HEADS, 2)),
            dma((KV_HEADS,)),
            dma((KV_HEADS,)),
            dma((KV_HEADS, 3, 2)),
            dma((KV_HEADS, 3, 2)),
        ],
        compiler_params=pltpu.CompilerParams(
            collective_id=0, has_side_effects=True, vmem_limit_bytes=40 * 1024 * 1024
        ),
        cost_estimate=pl.CostEstimate(
            flops=3_300_000_000, bytes_accessed=5_500_000, transcendentals=2_100_000
        ),
    )(*(pltpu.with_memory_space_constraint(x, pltpu.HBM) for x in (block_docs, queries, keys, values, out_grad)))
    return pl.pallas_call(
        write_out,
        out_shape=[pltpu.HBM(value.shape, value.dtype) for value in results],
        in_specs=[vmem] * 4,
        out_specs=[hbm] * 4,
        scratch_shapes=[dma((4,))],
    )(*(pltpu.with_memory_space_constraint(x, pltpu.VMEM) for x in results))


def solution(mesh):
    tokens = P(("seq", "ctx"), None)
    return jax.shard_map(
        on_device,
        mesh=mesh,
        in_specs=(tokens, tokens, tokens, tokens, P("seq")),
        out_specs=(tokens, tokens, tokens, tokens),
        check_vma=False,
    )
```

```python
import math

import jax
import jax.numpy as jnp
from jax import lax
from jax.experimental import pallas as pl
from jax.experimental.pallas import tpu as pltpu
from jax.sharding import PartitionSpec as P

HEAD_DIM = 128
HEADS = 16
KV_HEADS = 4
GROUP = HEADS // KV_HEADS
BLOCK = 128
MOST = 4
PIECES = 4
PIECE = 64
ROWS = 256
LEAD = (MOST - 1) * BLOCK
WINDOW = MOST * BLOCK
SCALE = 1.0 / math.sqrt(HEAD_DIM)
SCALE_LOG2 = math.log2(math.e) / math.sqrt(HEAD_DIM)
FAR = 1e30
MESH = pl.DeviceIdType.MESH

NT = (((1,), (1,)), ((), ()))
TN = (((0,), (0,)), ((), ()))
NN = (((1,), (0,)), ((), ()))


def dot(lhs, rhs, dims):
    return lax.dot_general(lhs, rhs, dims, preferred_element_type=jnp.float32)


def block_rows(value, index):
    return value[index * BLOCK : (index + 1) * BLOCK]


def attend(keys, values, queries, grads, live):
    width = queries.shape[0]
    scores = dot(keys, queries, NT)
    weight_grad = dot(values, grads, NT)
    causal = lax.broadcasted_iota(jnp.int32, (BLOCK, BLOCK), 0) <= lax.broadcasted_iota(
        jnp.int32, (BLOCK, BLOCK), 1
    )
    exps, inverses = [], []
    for lane in range(0, width, BLOCK):
        tiles = [block_rows(scores, t)[:, lane : lane + BLOCK] for t in range(MOST)]
        tiles[-1] = jnp.where(causal, tiles[-1], -FAR)
        top = jnp.max(tiles[-1], axis=0, keepdims=True)
        for t in range(MOST - 1):
            top = jnp.maximum(top, jnp.where(live[t], jnp.max(tiles[t], axis=0, keepdims=True), -FAR))
        top = top * SCALE_LOG2
        shifts = [jnp.where(live[t], top, FAR) for t in range(MOST - 1)] + [top]
        parts = [jnp.exp2(tiles[t] * SCALE_LOG2 - shifts[t]) for t in range(MOST)]
        inverses.append(1.0 / jnp.sum(sum(parts), axis=0, keepdims=True))
        exps.append(jnp.concatenate([p.astype(jnp.bfloat16) for p in parts], 0))
    exps = jnp.concatenate(exps, 1)
    inverse = jnp.concatenate(inverses, 1)
    attended = dot(values, exps, TN) * inverse
    row_dot = jnp.sum(attended * jnp.transpose(grads).astype(jnp.float32), axis=0, keepdims=True)
    score_grad = []
    for lane in range(0, width, BLOCK):
        lanes = slice(lane, lane + BLOCK)
        score_grad.append(
            jnp.concatenate(
                [
                    block_rows(exps, t)[:, lanes]
                    * (block_rows(weight_grad, t)[:, lanes] - row_dot[:, lanes]).astype(jnp.bfloat16)
                    for t in range(MOST)
                ],
                0,
            )
        )
    score_grad = jnp.concatenate(score_grad, 1)
    column = jnp.transpose(jnp.broadcast_to(inverse, (BLOCK, width)))
    value_part = dot(exps, (grads.astype(jnp.float32) * column).astype(jnp.bfloat16), NN)
    key_part = dot(score_grad, (queries.astype(jnp.float32) * column).astype(jnp.bfloat16), NN)

    def outputs():
        query_grad = dot(keys, score_grad, TN) * (inverse * SCALE)
        return (
            jnp.transpose(attended.astype(jnp.bfloat16)),
            jnp.transpose(query_grad.astype(jnp.bfloat16)),
        )

    return key_part * SCALE, value_part, outputs


def kernel(
    docs_hbm, q_hbm, k_hbm, v_hbm, g_hbm, att_buf, dq_buf, dk_buf, dv_buf,
    docs, q_buf, g_buf, kv_buf, part, own_part, send_buf, got_buf,
    load_sem, kv_sem,
    first_send, first_recv, own_send, own_recv, fwd_send, fwd_recv, ret_send, ret_recv,
):
    seq = lax.axis_index("seq")
    me = lax.axis_index("ctx")
    last = lax.axis_size("ctx") - 1
    has_prev, has_next = me > 0, me < last
    prev, following = jnp.maximum(me - 1, 0), jnp.minimum(me + 1, last)

    barrier = pltpu.get_barrier_semaphore()

    @pl.when(has_prev)
    def _():
        pl.semaphore_signal(barrier, inc=1, device_id=(seq, prev), device_id_type=MESH)

    kv_loads = []
    for h in range(KV_HEADS):
        for n, ref in enumerate((k_hbm, v_hbm)):
            copy = pltpu.make_async_copy(
                ref.at[:, pl.ds(h * HEAD_DIM, HEAD_DIM)],
                kv_buf.at[h, n, pl.ds(LEAD, ROWS)],
                kv_sem.at[h, n],
            )
            copy.start()
            kv_loads.append(copy)
    loads = [
        pltpu.make_async_copy(q_hbm, q_buf, load_sem.at[0]),
        pltpu.make_async_copy(g_hbm, g_buf, load_sem.at[1]),
        pltpu.make_async_copy(docs_hbm, docs, load_sem.at[2]),
    ]
    for copy in loads:
        copy.start()

    def own(h, b):
        return pltpu.make_async_remote_copy(
            kv_buf.at[h, :, pl.ds(LEAD + b * BLOCK, BLOCK)],
            kv_buf.at[h, :, pl.ds((1 + b) * BLOCK, BLOCK)],
            own_send.at[h, b], own_recv.at[h, b],
            device_id=(seq, following), device_id_type=MESH,
        )

    def first(p):
        n, rows = p // 2, p % 2 * PIECE
        return pltpu.make_async_remote_copy(
            (k_hbm, v_hbm)[n].at[pl.ds(BLOCK + rows, PIECE), pl.ds(0, HEAD_DIM)],
            kv_buf.at[0, n, pl.ds(2 * BLOCK + rows, PIECE)],
            first_send.at[p], first_recv.at[p],
            device_id=(seq, following), device_id_type=MESH,
        )

    def forward(h):
        return pltpu.make_async_remote_copy(
            kv_buf.at[h, :, pl.ds(2 * BLOCK, BLOCK)],
            kv_buf.at[h, :, pl.ds(0, BLOCK)],
            fwd_send.at[h], fwd_recv.at[h],
            device_id=(seq, following), device_id_type=MESH,
        )

    def forward_first(p):
        n, rows = p // 2, p % 2 * PIECE
        return pltpu.make_async_remote_copy(
            kv_buf.at[0, n, pl.ds(2 * BLOCK + rows, PIECE)],
            kv_buf.at[0, n, pl.ds(rows, PIECE)],
            first_send.at[PIECES + p], first_recv.at[PIECES + p],
            device_id=(seq, following), device_id_type=MESH,
        )

    def give_back(h, b, n):
        return pltpu.make_async_remote_copy(
            send_buf.at[h, b, n], got_buf.at[h, b, n],
            ret_send.at[h, b, n], ret_recv.at[h, b, n],
            device_id=(seq, prev), device_id_type=MESH,
        )

    def give_back_b(h):
        return pltpu.make_async_remote_copy(
            send_buf.at[h, 1], got_buf.at[h, 1],
            ret_send.at[h, 1, 0], ret_recv.at[h, 1, 0],
            device_id=(seq, prev), device_id_type=MESH,
        )

    def next_first(h):
        @pl.when(has_next)
        def _():
            own(h, 1).start()

    def next_second(h):
        @pl.when(has_next)
        def _():
            own(h, 0).start()

    @pl.when(has_next)
    def _():
        pl.semaphore_wait(barrier, 1)
        for p in range(PIECES):
            first(p).start()

    for copy in kv_loads:
        copy.wait()


    @pl.when(jnp.logical_not(has_prev))
    def _():
        kv_buf[:, :, :LEAD] = jnp.zeros((KV_HEADS, 2, LEAD, HEAD_DIM), jnp.bfloat16)

    for copy in loads:
        copy.wait()

    def live(slot):
        own_doc = docs[2 * me + slot]
        result = []
        for t in range(MOST - 1):
            place = 2 * me + slot + t - (MOST - 1)
            result.append((place >= 0) & (docs[jnp.maximum(place, 0)] == own_doc))
        return result

    lives = [live(0), live(1)]

    def compute(h, slot):
        rows = slice(slot * BLOCK, (slot + 1) * BLOCK)
        lanes = [slice((h * GROUP + j) * HEAD_DIM, (h * GROUP + j + 1) * HEAD_DIM) for j in range(GROUP)]
        queries = jnp.concatenate([q_buf[rows, lane] for lane in lanes], 0)
        grads = jnp.concatenate([g_buf[rows, lane] for lane in lanes], 0)
        keys = kv_buf[h, 0, slot * BLOCK : slot * BLOCK + WINDOW]
        values = kv_buf[h, 1, slot * BLOCK : slot * BLOCK + WINDOW]
        key_part, value_part, outputs = attend(keys, values, queries, grads, lives[slot])

        def write():
            attended, query_grad = outputs()
            for j, lane in enumerate(lanes):
                att_buf[rows, lane] = block_rows(attended, j)
                dq_buf[rows, lane] = block_rows(query_grad, j)

        return (key_part, value_part), write

    def relay(h):
        @pl.when(has_next)
        def _():
            for n in (1, 0):
                give_back(h, 0, n).wait_recv()
                send_buf[h, 2, n] = (part[h, n] + got_buf[h, 0, n].astype(jnp.float32)).astype(jnp.bfloat16)

                @pl.when(has_prev)
                def _(n=n):
                    give_back(h, 2, n).start()

        @pl.when(jnp.logical_not(has_next))
        def _():
            send_buf[h, 2] = part[h].astype(jnp.bfloat16)
            for n in (1, 0):
                give_back(h, 2, n).start()

    def finish(h):
        @pl.when(has_next)
        def _():
            give_back_b(h).wait_recv()
            for n in range(2):
                give_back(h, 2, n).wait_recv()
            for b in range(2):
                own_part[h, b] += got_buf[h, 1 + b].astype(jnp.float32)

        for n, ref in enumerate((dk_buf, dv_buf)):
            for b in range(2):
                ref[b * BLOCK : (b + 1) * BLOCK, h * HEAD_DIM : (h + 1) * HEAD_DIM] = own_part[
                    h, b, n
                ].astype(jnp.bfloat16)

    def pass_on(h):
        if h == 0:
            for p in range(PIECES):

                @pl.when(has_prev)
                def _(p=p):
                    first(p).wait_recv()

                @pl.when(has_next)
                def _(p=p):
                    forward_first(p).start()
        else:

            @pl.when(has_prev)
            def _():
                own(h, 1).wait_recv()

            @pl.when(has_next)
            def _():
                forward(h).start()

    unwritten = {}

    def write_one(h):
        unwritten.pop((h, 1))()

    def write_zero(h):
        unwritten.pop((h, 0))()

    def slot_one(h):
        @pl.when(has_prev)
        def _():
            own(h, 0).wait_recv()

        sums, write = compute(h, 1)
        for n in range(2):
            part[h, n] = block_rows(sums[n], 1)
            own_part[h, 0, n] = block_rows(sums[n], 2)
            own_part[h, 1, n] = block_rows(sums[n], 3)
            own_part[h, 2, n] = block_rows(sums[n], 0)
        unwritten[h, 1] = write

    def slot_zero(h):
        @pl.when(has_prev)
        def _():
            if h == 0:
                for p in range(PIECES):
                    forward_first(p).wait_recv()
            else:
                forward(h).wait_recv()

        sums, write = compute(h, 0)
        for n in range(2):
            send_buf[h, 0, n] = block_rows(sums[n], 0).astype(jnp.bfloat16)
            send_buf[h, 1, n] = (block_rows(sums[n], 1) + own_part[h, 2, n]).astype(jnp.bfloat16)

        @pl.when(has_prev)
        def _():
            for n in (1, 0):
                give_back(h, 0, n).start()
            give_back_b(h).start()

        for n in range(2):
            part[h, n] += block_rows(sums[n], 2)
            own_part[h, 0, n] += block_rows(sums[n], 3)
        unwritten[h, 0] = write

    def drain(h):
        @pl.when(has_next)
        def _():
            for p in range(PIECES):
                first(p).wait_send()
                forward_first(p).wait_send()
            for g in range(KV_HEADS):
                own(g, 0).wait_send()
                if g > 0:
                    own(g, 1).wait_send()
                    forward(g).wait_send()

        @pl.when(has_prev)
        def _():
            for g in range(KV_HEADS):
                give_back_b(g).wait_send()
                for b in (0,) if g == h else (0, 2):
                    for n in range(2):
                        give_back(g, b, n).wait_send()

    order = (
        (next_first, 1),
        (next_second, 0),
        (pass_on, 0),
        (next_second, 1),
        (pass_on, 1),
        (slot_one, 0),
        (write_one, 0),
        (next_first, 2),
        (slot_zero, 0),
        (next_first, 3),
        (next_second, 2),
        (slot_one, 1),
        (slot_zero, 1),
        (pass_on, 2),
        (write_one, 1),
        (next_second, 3),
        (relay, 0),
        (pass_on, 3),
        (slot_one, 2),
        (relay, 1),
        (slot_zero, 2),
        (write_one, 2),
        (slot_one, 3),
        (slot_zero, 3),
        (write_zero, 0),
        (write_one, 3),
        (finish, 1),
        (write_zero, 3),
        (write_zero, 1),
        (finish, 0),
        (relay, 2),
        (relay, 3),
        (drain, 3),
        (finish, 2),
        (write_zero, 2),
        (finish, 3),
    )
    for step, h in order:
        step(h)

    final = KV_HEADS - 1

    @pl.when(has_prev)
    def _():
        for n in range(2):
            give_back(final, 2, n).wait_send()


def write_out(*refs):
    count = len(refs) // 2
    sem = refs[-1]
    copies = [pltpu.make_async_copy(refs[n], refs[count + n], sem.at[n]) for n in range(count)]
    for copy in copies:
        copy.start()
    for copy in copies:
        copy.wait()


def on_device(queries, keys, values, out_grad, block_docs):
    hbm = pl.BlockSpec(memory_space=pl.ANY)
    dma = pltpu.SemaphoreType.DMA
    bf16, f32 = jnp.bfloat16, jnp.float32
    vmem = pl.BlockSpec(memory_space=pltpu.VMEM)
    results = pl.pallas_call(
        kernel,
        out_shape=[
            pltpu.VMEM(queries.shape, bf16),
            pltpu.VMEM(queries.shape, bf16),
            pltpu.VMEM(keys.shape, bf16),
            pltpu.VMEM(keys.shape, bf16),
        ],
        in_specs=[hbm] * 5,
        out_specs=[vmem] * 4,
        scratch_shapes=[
            pltpu.SMEM(block_docs.shape, jnp.int32),
            pltpu.VMEM((ROWS, HEADS * HEAD_DIM), bf16),
            pltpu.VMEM((ROWS, HEADS * HEAD_DIM), bf16),
            pltpu.VMEM((KV_HEADS, 2, LEAD + ROWS, HEAD_DIM), bf16),
            pltpu.VMEM((KV_HEADS, 2, BLOCK, HEAD_DIM), f32),
            pltpu.VMEM((KV_HEADS, 3, 2, BLOCK, HEAD_DIM), f32),
            pltpu.VMEM((KV_HEADS, 3, 2, BLOCK, HEAD_DIM), bf16),
            pltpu.VMEM((KV_HEADS, 3, 2, BLOCK, HEAD_DIM), bf16),
            dma((3,)),
            dma((KV_HEADS, 2)),
            dma((2 * PIECES,)),
            dma((2 * PIECES,)),
            dma((KV_HEADS, 2)),
            dma((KV_HEADS, 2)),
            dma((KV_HEADS,)),
            dma((KV_HEADS,)),
            dma((KV_HEADS, 3, 2)),
            dma((KV_HEADS, 3, 2)),
        ],
        compiler_params=pltpu.CompilerParams(
            collective_id=0, has_side_effects=True, vmem_limit_bytes=40 * 1024 * 1024
        ),
        cost_estimate=pl.CostEstimate(
            flops=3_300_000_000, bytes_accessed=5_500_000, transcendentals=2_100_000
        ),
    )(*(pltpu.with_memory_space_constraint(x, pltpu.HBM) for x in (block_docs, queries, keys, values, out_grad)))
    return pl.pallas_call(
        write_out,
        out_shape=[pltpu.HBM(value.shape, value.dtype) for value in results],
        in_specs=[vmem] * 4,
        out_specs=[hbm] * 4,
        scratch_shapes=[dma((4,))],
    )(*(pltpu.with_memory_space_constraint(x, pltpu.VMEM) for x in results))


def solution(mesh):
    tokens = P(("seq", "ctx"), None)
    return jax.shard_map(
        on_device,
        mesh=mesh,
        in_specs=(tokens, tokens, tokens, tokens, P("seq")),
        out_specs=(tokens, tokens, tokens, tokens),
        check_vma=False,
    )
```

```python
import math

import jax
import jax.numpy as jnp
from jax import lax
from jax.experimental import pallas as pl
from jax.experimental.pallas import tpu as pltpu
from jax.sharding import PartitionSpec as P

HEAD_DIM = 128
HEADS = 16
KV_HEADS = 4
GROUP = HEADS // KV_HEADS
BLOCK = 128
MOST = 4
PIECES = 4
PIECE = 64
ROWS = 256
LEAD = (MOST - 1) * BLOCK
WINDOW = MOST * BLOCK
SCALE = 1.0 / math.sqrt(HEAD_DIM)
SCALE_LOG2 = math.log2(math.e) / math.sqrt(HEAD_DIM)
FAR = 1e30
MESH = pl.DeviceIdType.MESH

NT = (((1,), (1,)), ((), ()))
TN = (((0,), (0,)), ((), ()))
NN = (((1,), (0,)), ((), ()))


def dot(lhs, rhs, dims):
    return lax.dot_general(lhs, rhs, dims, preferred_element_type=jnp.float32)


def block_rows(value, index):
    return value[index * BLOCK : (index + 1) * BLOCK]


def attend(keys, values, queries, grads, live):
    width = queries.shape[0]
    scores = dot(keys, queries, NT)
    weight_grad = dot(values, grads, NT)
    causal = lax.broadcasted_iota(jnp.int32, (BLOCK, BLOCK), 0) <= lax.broadcasted_iota(
        jnp.int32, (BLOCK, BLOCK), 1
    )
    exps, inverses = [], []
    for lane in range(0, width, BLOCK):
        tiles = [block_rows(scores, t)[:, lane : lane + BLOCK] for t in range(MOST)]
        tiles[-1] = jnp.where(causal, tiles[-1], -FAR)
        top = jnp.max(tiles[-1], axis=0, keepdims=True)
        for t in range(MOST - 1):
            top = jnp.maximum(top, jnp.where(live[t], jnp.max(tiles[t], axis=0, keepdims=True), -FAR))
        top = top * SCALE_LOG2
        shifts = [jnp.where(live[t], top, FAR) for t in range(MOST - 1)] + [top]
        parts = [jnp.exp2(tiles[t] * SCALE_LOG2 - shifts[t]) for t in range(MOST)]
        inverses.append(1.0 / jnp.sum(sum(parts), axis=0, keepdims=True))
        exps.append(jnp.concatenate([p.astype(jnp.bfloat16) for p in parts], 0))
    exps = jnp.concatenate(exps, 1)
    inverse = jnp.concatenate(inverses, 1)
    attended = dot(values, exps, TN) * inverse
    row_dot = jnp.sum(attended * jnp.transpose(grads).astype(jnp.float32), axis=0, keepdims=True)
    score_grad = []
    for lane in range(0, width, BLOCK):
        lanes = slice(lane, lane + BLOCK)
        score_grad.append(
            jnp.concatenate(
                [
                    block_rows(exps, t)[:, lanes]
                    * (block_rows(weight_grad, t)[:, lanes] - row_dot[:, lanes]).astype(jnp.bfloat16)
                    for t in range(MOST)
                ],
                0,
            )
        )
    score_grad = jnp.concatenate(score_grad, 1)
    column = jnp.transpose(jnp.broadcast_to(inverse, (BLOCK, width)))
    value_part = dot(exps, (grads.astype(jnp.float32) * column).astype(jnp.bfloat16), NN)
    key_part = dot(score_grad, (queries.astype(jnp.float32) * column).astype(jnp.bfloat16), NN)

    def outputs():
        query_grad = dot(keys, score_grad, TN) * (inverse * SCALE)
        return (
            jnp.transpose(attended.astype(jnp.bfloat16)),
            jnp.transpose(query_grad.astype(jnp.bfloat16)),
        )

    return key_part * SCALE, value_part, outputs


def kernel(
    docs_hbm, q_hbm, k_hbm, v_hbm, g_hbm, att_buf, dq_buf, dk_buf, dv_buf,
    docs, q_buf, g_buf, kv_buf, part, own_part, send_buf, got_buf,
    load_sem, kv_sem,
    first_send, first_recv, own_send, own_recv, fwd_send, fwd_recv, ret_send, ret_recv,
):
    seq = lax.axis_index("seq")
    me = lax.axis_index("ctx")
    last = lax.axis_size("ctx") - 1
    has_prev, has_next = me > 0, me < last
    prev, following = jnp.maximum(me - 1, 0), jnp.minimum(me + 1, last)

    barrier = pltpu.get_barrier_semaphore()

    @pl.when(has_prev)
    def _():
        pl.semaphore_signal(barrier, inc=1, device_id=(seq, prev), device_id_type=MESH)

    kv_loads = []
    for h in range(KV_HEADS):
        for n, ref in enumerate((k_hbm, v_hbm)):
            copy = pltpu.make_async_copy(
                ref.at[:, pl.ds(h * HEAD_DIM, HEAD_DIM)],
                kv_buf.at[h, n, pl.ds(LEAD, ROWS)],
                kv_sem.at[h, n],
            )
            copy.start()
            kv_loads.append(copy)
    loads = [
        pltpu.make_async_copy(q_hbm, q_buf, load_sem.at[0]),
        pltpu.make_async_copy(g_hbm, g_buf, load_sem.at[1]),
        pltpu.make_async_copy(docs_hbm, docs, load_sem.at[2]),
    ]
    for copy in loads:
        copy.start()

    def own(h, b):
        return pltpu.make_async_remote_copy(
            kv_buf.at[h, :, pl.ds(LEAD + b * BLOCK, BLOCK)],
            kv_buf.at[h, :, pl.ds((1 + b) * BLOCK, BLOCK)],
            own_send.at[h, b], own_recv.at[h, b],
            device_id=(seq, following), device_id_type=MESH,
        )

    def first(p):
        n, rows = p // 2, p % 2 * PIECE
        return pltpu.make_async_remote_copy(
            (k_hbm, v_hbm)[n].at[pl.ds(BLOCK + rows, PIECE), pl.ds(0, HEAD_DIM)],
            kv_buf.at[0, n, pl.ds(2 * BLOCK + rows, PIECE)],
            first_send.at[p], first_recv.at[p],
            device_id=(seq, following), device_id_type=MESH,
        )

    def forward(h):
        return pltpu.make_async_remote_copy(
            kv_buf.at[h, :, pl.ds(2 * BLOCK, BLOCK)],
            kv_buf.at[h, :, pl.ds(0, BLOCK)],
            fwd_send.at[h], fwd_recv.at[h],
            device_id=(seq, following), device_id_type=MESH,
        )

    def forward_first(p):
        n, rows = p // 2, p % 2 * PIECE
        return pltpu.make_async_remote_copy(
            kv_buf.at[0, n, pl.ds(2 * BLOCK + rows, PIECE)],
            kv_buf.at[0, n, pl.ds(rows, PIECE)],
            first_send.at[PIECES + p], first_recv.at[PIECES + p],
            device_id=(seq, following), device_id_type=MESH,
        )

    def give_back(h, b, n):
        return pltpu.make_async_remote_copy(
            send_buf.at[h, b, n], got_buf.at[h, b, n],
            ret_send.at[h, b, n], ret_recv.at[h, b, n],
            device_id=(seq, prev), device_id_type=MESH,
        )

    def next_first(h):
        @pl.when(has_next)
        def _():
            own(h, 1).start()

    def next_second(h):
        @pl.when(has_next)
        def _():
            own(h, 0).start()

    @pl.when(has_next)
    def _():
        pl.semaphore_wait(barrier, 1)
        for p in range(PIECES):
            first(p).start()

    for copy in kv_loads:
        copy.wait()


    @pl.when(jnp.logical_not(has_prev))
    def _():
        kv_buf[:, :, :LEAD] = jnp.zeros((KV_HEADS, 2, LEAD, HEAD_DIM), jnp.bfloat16)

    for copy in loads:
        copy.wait()

    def live(slot):
        own_doc = docs[2 * me + slot]
        result = []
        for t in range(MOST - 1):
            place = 2 * me + slot + t - (MOST - 1)
            result.append((place >= 0) & (docs[jnp.maximum(place, 0)] == own_doc))
        return result

    lives = [live(0), live(1)]

    def compute(h, slot):
        rows = slice(slot * BLOCK, (slot + 1) * BLOCK)
        lanes = [slice((h * GROUP + j) * HEAD_DIM, (h * GROUP + j + 1) * HEAD_DIM) for j in range(GROUP)]
        queries = jnp.concatenate([q_buf[rows, lane] for lane in lanes], 0)
        grads = jnp.concatenate([g_buf[rows, lane] for lane in lanes], 0)
        keys = kv_buf[h, 0, slot * BLOCK : slot * BLOCK + WINDOW]
        values = kv_buf[h, 1, slot * BLOCK : slot * BLOCK + WINDOW]
        key_part, value_part, outputs = attend(keys, values, queries, grads, lives[slot])

        def write():
            attended, query_grad = outputs()
            for j, lane in enumerate(lanes):
                att_buf[rows, lane] = block_rows(attended, j)
                dq_buf[rows, lane] = block_rows(query_grad, j)

        return (key_part, value_part), write

    def relay(h):
        @pl.when(has_next)
        def _():
            for n in (1, 0):
                give_back(h, 0, n).wait_recv()
                send_buf[h, 2, n] = (part[h, n] + got_buf[h, 0, n].astype(jnp.float32)).astype(jnp.bfloat16)

                @pl.when(has_prev)
                def _(n=n):
                    give_back(h, 2, n).start()

        @pl.when(jnp.logical_not(has_next))
        def _():
            send_buf[h, 2] = part[h].astype(jnp.bfloat16)
            for n in (1, 0):
                give_back(h, 2, n).start()

    def finish(h):
        @pl.when(has_next)
        def _():
            for b in range(2):
                for n in range(2):
                    give_back(h, 1 + b, n).wait_recv()
                own_part[h, b] += got_buf[h, 1 + b].astype(jnp.float32)

        for n, ref in enumerate((dk_buf, dv_buf)):
            for b in range(2):
                ref[b * BLOCK : (b + 1) * BLOCK, h * HEAD_DIM : (h + 1) * HEAD_DIM] = own_part[
                    h, b, n
                ].astype(jnp.bfloat16)

    def pass_on(h):
        if h == 0:
            for p in range(PIECES):

                @pl.when(has_prev)
                def _(p=p):
                    first(p).wait_recv()

                @pl.when(has_next)
                def _(p=p):
                    forward_first(p).start()
        else:

            @pl.when(has_prev)
            def _():
                own(h, 1).wait_recv()

            @pl.when(has_next)
            def _():
                forward(h).start()

    unwritten = {}

    def write_one(h):
        unwritten.pop((h, 1))()

    def write_zero(h):
        unwritten.pop((h, 0))()

    def slot_one(h):
        @pl.when(has_prev)
        def _():
            own(h, 0).wait_recv()

        sums, write = compute(h, 1)
        for n in range(2):
            part[h, n] = block_rows(sums[n], 1)
            own_part[h, 0, n] = block_rows(sums[n], 2)
            own_part[h, 1, n] = block_rows(sums[n], 3)
            own_part[h, 2, n] = block_rows(sums[n], 0)
        unwritten[h, 1] = write

    def slot_zero(h):
        @pl.when(has_prev)
        def _():
            if h == 0:
                for p in range(PIECES):
                    forward_first(p).wait_recv()
            else:
                forward(h).wait_recv()

        sums, write = compute(h, 0)
        for n in range(2):
            send_buf[h, 0, n] = block_rows(sums[n], 0).astype(jnp.bfloat16)
            send_buf[h, 1, n] = (block_rows(sums[n], 1) + own_part[h, 2, n]).astype(jnp.bfloat16)

        @pl.when(has_prev)
        def _():
            for b in range(2):
                for n in (1, 0):
                    give_back(h, b, n).start()

        for n in range(2):
            part[h, n] += block_rows(sums[n], 2)
            own_part[h, 0, n] += block_rows(sums[n], 3)
        unwritten[h, 0] = write

    order = (
        (next_first, 1),
        (next_second, 0),
        (pass_on, 0),
        (next_second, 1),
        (pass_on, 1),
        (slot_one, 0),
        (write_one, 0),
        (next_first, 2),
        (slot_zero, 0),
        (next_first, 3),
        (next_second, 2),
        (slot_one, 1),
        (slot_zero, 1),
        (pass_on, 2),
        (write_one, 1),
        (next_second, 3),
        (relay, 0),
        (pass_on, 3),
        (slot_one, 2),
        (relay, 1),
        (slot_zero, 2),
        (slot_one, 3),
        (slot_zero, 3),
        (relay, 2),
        (write_one, 2),
        (write_one, 3),
        (write_zero, 0),
        (finish, 1),
        (write_zero, 3),
        (write_zero, 1),
        (finish, 0),
        (relay, 3),
        (finish, 2),
        (write_zero, 2),
        (finish, 3),
    )
    for step, h in order:
        step(h)

    @pl.when(has_next)
    def _():
        for p in range(PIECES):
            first(p).wait_send()
            forward_first(p).wait_send()
        for h in range(KV_HEADS):
            own(h, 0).wait_send()
            if h > 0:
                own(h, 1).wait_send()
                forward(h).wait_send()

    @pl.when(has_prev)
    def _():
        for h in range(KV_HEADS):
            for b in range(3):
                for n in range(2):
                    give_back(h, b, n).wait_send()

def write_out(*refs):
    count = len(refs) // 2
    sem = refs[-1]
    copies = [pltpu.make_async_copy(refs[n], refs[count + n], sem.at[n]) for n in range(count)]
    for copy in copies:
        copy.start()
    for copy in copies:
        copy.wait()


def on_device(queries, keys, values, out_grad, block_docs):
    hbm = pl.BlockSpec(memory_space=pl.ANY)
    dma = pltpu.SemaphoreType.DMA
    bf16, f32 = jnp.bfloat16, jnp.float32
    vmem = pl.BlockSpec(memory_space=pltpu.VMEM)
    results = pl.pallas_call(
        kernel,
        out_shape=[
            pltpu.VMEM(queries.shape, bf16),
            pltpu.VMEM(queries.shape, bf16),
            pltpu.VMEM(keys.shape, bf16),
            pltpu.VMEM(keys.shape, bf16),
        ],
        in_specs=[hbm] * 5,
        out_specs=[vmem] * 4,
        scratch_shapes=[
            pltpu.SMEM(block_docs.shape, jnp.int32),
            pltpu.VMEM((ROWS, HEADS * HEAD_DIM), bf16),
            pltpu.VMEM((ROWS, HEADS * HEAD_DIM), bf16),
            pltpu.VMEM((KV_HEADS, 2, LEAD + ROWS, HEAD_DIM), bf16),
            pltpu.VMEM((KV_HEADS, 2, BLOCK, HEAD_DIM), f32),
            pltpu.VMEM((KV_HEADS, 3, 2, BLOCK, HEAD_DIM), f32),
            pltpu.VMEM((KV_HEADS, 3, 2, BLOCK, HEAD_DIM), bf16),
            pltpu.VMEM((KV_HEADS, 3, 2, BLOCK, HEAD_DIM), bf16),
            dma((3,)),
            dma((KV_HEADS, 2)),
            dma((2 * PIECES,)),
            dma((2 * PIECES,)),
            dma((KV_HEADS, 2)),
            dma((KV_HEADS, 2)),
            dma((KV_HEADS,)),
            dma((KV_HEADS,)),
            dma((KV_HEADS, 3, 2)),
            dma((KV_HEADS, 3, 2)),
        ],
        compiler_params=pltpu.CompilerParams(
            collective_id=0, has_side_effects=True, vmem_limit_bytes=40 * 1024 * 1024
        ),
        cost_estimate=pl.CostEstimate(
            flops=3_300_000_000, bytes_accessed=5_500_000, transcendentals=2_100_000
        ),
    )(*(pltpu.with_memory_space_constraint(x, pltpu.HBM) for x in (block_docs, queries, keys, values, out_grad)))
    return pl.pallas_call(
        write_out,
        out_shape=[pltpu.HBM(value.shape, value.dtype) for value in results],
        in_specs=[vmem] * 4,
        out_specs=[hbm] * 4,
        scratch_shapes=[dma((4,))],
    )(*(pltpu.with_memory_space_constraint(x, pltpu.VMEM) for x in results))


def solution(mesh):
    tokens = P(("seq", "ctx"), None)
    return jax.shard_map(
        on_device,
        mesh=mesh,
        in_specs=(tokens, tokens, tokens, tokens, P("seq")),
        out_specs=(tokens, tokens, tokens, tokens),
        check_vma=False,
    )
```
